256 devices in a mesh: hid: 64 (over y, z_lo, x), mdl: 4 (over z_hi, core).
Axes of the slice: x: 4, y: 4, z: 8 (z_hi: 2, z_lo: 4; z = z_hi * 4 + z_lo), core: 2. Of those that a mesh axis runs over, the one named last changes fastest.
Arguments:
- quant_input: bfloat16 [512, 8192], P('hid', 'mdl'), may hold values from -4 to 4
- input_scale: float32 [512], P('hid'), may hold values from 0.25 to 4
- grad_output: bfloat16 [512, 8192], P('hid', 'mdl'), may hold values from -0.625 to 0.625
- gate_quant: bfloat16 [8192, 28672], P('mdl', 'hid'), may hold values from -0.0625 to 0.0625
- gate_scale: float32 [28672], P('hid'), may hold values from 0.5 to 2
- up_quant: bfloat16 [8192, 28672], P('mdl', 'hid'), may hold values from -0.0625 to 0.0625
- up_scale: float32 [28672], P('hid'), may hold values from 0.5 to 2
- down_quant: bfloat16 [28672, 8192], P('hid', 'mdl'), may hold values from -0.0625 to 0.0625
- down_scale: float32 [28672], P('hid'), may hold values from 0.5 to 2
Outputs:
- input_grad: bfloat16 [512, 8192], P('hid', 'mdl')
- gate_grad: bfloat16 [8192, 28672], P('mdl', 'hid')
- up_grad: bfloat16 [8192, 28672], P('mdl', 'hid')
- down_grad: bfloat16 [28672, 8192], P('hid', 'mdl')
The draws below stay inside these ranges and needn't reach their ends.
All inputs are finite; a program needn't handle non-finite values.
Results may differ from the reference program's by a relative error of at most 0.0092.
Values may be sent and summed in bfloat16 or wider, within the bound.
A program may use at most 64 MiB of HBM per device.

```python
import math
import jax
import jax.numpy as jnp
from jax import lax

D = 8192
FF = 28672
TOKENS = 512
N_HID = 64


def steps_of(own_key, shape, split, low, largest):
    level, own = 1.0, jax.random.fold_in(own_key, 6)
    for position, blocks in split:
        heights = jnp.exp(jax.random.uniform(jax.random.fold_in(own, position), (blocks,), jnp.float32, low / len(split), largest / len(split)))
        level = level * jnp.repeat(heights, shape[position] // blocks).reshape([-1 if axis == position else 1 for axis in range(len(shape))])
    return level


def bell_draw(own_key, extent, deviation, reach, split=(), kind=jnp.bfloat16):
    factor_of = steps_of(own_key, extent, split, -0.22, 0.18) if split else 1.0
    entries = jax.random.normal(own_key, extent, jnp.float32) * deviation * factor_of
    return jnp.minimum(jnp.maximum(entries, -reach), reach).astype(kind)


def setup_inputs(seed: int = 0) -> dict:
    seeds = jax.random.split(jax.random.key(seed), 10)
    quant_input = bell_draw(seeds[0], (TOKENS, D), 1.0, 4.0, ((0, 64), (1, 4)))
    input_scale = jnp.clip(jnp.exp(math.log(4.0) - 2.7725887 * jax.random.uniform(seeds[1], (TOKENS,), jnp.float32) ** steps_of(seeds[1], (TOKENS,), ((0, 64),), -0.2, 0.2)), 0.25, 4.0)
    grad_output = bell_draw(seeds[2], (TOKENS, D), 0.1, 0.625, ((0, 64), (1, 4)))
    gate_quant = bell_draw(seeds[3], (D, FF), D ** -0.5, 0.0625, ((0, 4), (1, 64)))
    gate_scale = jnp.clip(jnp.exp(math.log(2.0) - 1.3862944 * jax.random.uniform(seeds[4], (FF,), jnp.float32) ** steps_of(seeds[4], (FF,), ((0, 64),), -0.2, 0.2)), 0.5, 2.0)
    up_quant = bell_draw(seeds[5], (D, FF), D ** -0.5, 0.0625, ((0, 4), (1, 64)))
    up_scale = jnp.clip(jnp.exp(math.log(2.0) - 1.3862944 * jax.random.uniform(seeds[6], (FF,), jnp.float32) ** steps_of(seeds[6], (FF,), ((0, 64),), -0.2, 0.2)), 0.5, 2.0)
    down_quant = bell_draw(seeds[7], (FF, D), D ** -0.5, 0.0625, ((0, 64), (1, 4)))
    down_scale = jnp.clip(jnp.exp(math.log(2.0) - 1.3862944 * jax.random.uniform(seeds[8], (FF,), jnp.float32) ** steps_of(seeds[8], (FF,), ((0, 64),), -0.2, 0.2)), 0.5, 2.0)
    return dict(quant_input=quant_input, input_scale=input_scale, grad_output=grad_output, gate_quant=gate_quant, gate_scale=gate_scale, up_quant=up_quant, up_scale=up_scale, down_quant=down_quant, down_scale=down_scale)


def reference(quant_input, input_scale, grad_output, gate_quant, gate_scale, up_quant, up_scale, down_quant, down_scale):
    activations = (quant_input.astype(jnp.float32) * input_scale[:, None]).astype(jnp.bfloat16)
    width = FF // N_HID
    blocks = FF // width

    def block(carry, block_index):
        start = (block_index * width).astype(jnp.int32)
        gate_weight = (lax.dynamic_slice_in_dim(gate_quant, start, width, 1).astype(jnp.float32) * lax.dynamic_slice_in_dim(gate_scale, start, width, 0)).astype(jnp.bfloat16)
        up_weight = (lax.dynamic_slice_in_dim(up_quant, start, width, 1).astype(jnp.float32) * lax.dynamic_slice_in_dim(up_scale, start, width, 0)).astype(jnp.bfloat16)
        down_weight = (lax.dynamic_slice_in_dim(down_quant, start, width, 0).astype(jnp.float32) * lax.dynamic_slice_in_dim(down_scale, start, width, 0)[:, None]).astype(jnp.bfloat16)
        gate_sum = jnp.dot(activations, gate_weight, preferred_element_type=jnp.float32)
        up_sum = jnp.dot(activations, up_weight, preferred_element_type=jnp.float32)
        hidden_grad = jnp.dot(grad_output, down_weight.T, preferred_element_type=jnp.float32)
        gate_sigmoid = jax.nn.sigmoid(gate_sum)
        hidden = (gate_sum * gate_sigmoid * up_sum).astype(jnp.bfloat16)
        gate_delta = (hidden_grad * up_sum * gate_sigmoid * (1.0 + gate_sum * (1.0 - gate_sigmoid))).astype(jnp.bfloat16)
        up_delta = (hidden_grad * gate_sum * gate_sigmoid).astype(jnp.bfloat16)
        carry = carry + jnp.dot(gate_delta, gate_weight.T, preferred_element_type=jnp.float32) + jnp.dot(up_delta, up_weight.T, preferred_element_type=jnp.float32)
        gate_piece = jnp.dot(activations.T, gate_delta, preferred_element_type=jnp.float32).astype(jnp.bfloat16)
        up_piece = jnp.dot(activations.T, up_delta, preferred_element_type=jnp.float32).astype(jnp.bfloat16)
        down_piece = jnp.dot(hidden.T, grad_output, preferred_element_type=jnp.float32).astype(jnp.bfloat16)
        return carry, (gate_piece, up_piece, down_piece)

    initial = jnp.zeros((TOKENS, D), jnp.float32)
    total, pieces = lax.scan(block, initial, jnp.arange(blocks, dtype=jnp.int32))
    gate_grad = jnp.transpose(pieces[0], (1, 0, 2)).reshape(D, FF)
    up_grad = jnp.transpose(pieces[1], (1, 0, 2)).reshape(D, FF)
    down_grad = pieces[2].reshape(FF, D)
    return total.astype(jnp.bfloat16), gate_grad, up_grad, down_grad
```

```python
import jax
import jax.numpy as jnp
from jax import lax
from jax.experimental import pallas as pl
from jax.experimental.pallas import tpu as pltpu
from jax.sharding import PartitionSpec as P

MESH = pl.DeviceIdType.MESH
BF = jnp.bfloat16
F32 = jnp.float32
D = 2048
H = 448
HP = 512
TOKENS = 512


def contract_rows(left, right):
    return lax.dot_general(left, right, (((0,), (0,)), ((), ())), preferred_element_type=F32)


def contract_cols(left, right):
    return lax.dot_general(left, right, (((1,), (1,)), ((), ())), preferred_element_type=F32)


def rows_at(start, size, step):
    return pl.ds(pl.multiple_of(start, step), size)


def kernel(
    slab, gate_q, up_q, down_q, gate_s, up_s, down_s,
    dx, act, grad, delta, hidden,
    gathered, raw_g, raw_u, raw_d, w_gu, w_d, part, sib, total, z_out, z_in,
    pi_own, pi_out, r1_in, r2_own, r2_out, r2_in, r3_own, r3_out, r3_in,
    load_sem, gz, gp, gn, gf, sc, sz, sd, s1, s2, s3,
):
    hid = lax.axis_index("hid")
    mdl = lax.axis_index("mdl")
    x, z, y = hid % 4, (hid // 4) % 4, hid // 16
    core, half = mdl % 2, mdl // 2

    def at(px, py, pz):
        return ((py * 4 + pz) * 4 + px, mdl)

    def x_peer(d):
        return at((x + d) % 4, y, z)

    def y_peer(d):
        return at(x, (y + d) % 4, z)

    def z_peer(d):
        return at(x, y, (z + d) % 4)

    sibling = (hid, half * 2 + (1 - core))
    far = (hid, (1 - half) * 2 + core)

    pos = jnp.where(z < 2, (y * 4 + x) * 2 + z, 32 + (x * 4 + y) * 2 + z - 2)
    loads = [
        pltpu.make_async_copy(src, dst, load_sem.at[i])
        for i, (src, dst) in enumerate(
            [(gate_q, raw_g), (up_q, raw_u), (down_q, raw_d), (slab, gathered.at[pos])]
        )
    ]
    for c in (loads[3], loads[0], loads[1], loads[2]):
        c.start()

    barrier = pltpu.get_barrier_semaphore()
    partners = [f(d) for f in (x_peer, y_peer, z_peer) for d in (1, 2, 3)] + [sibling, far]
    for p in partners:
        pl.semaphore_signal(barrier, inc=1, device_id=p, device_id_type=MESH)
    pl.semaphore_wait(barrier, len(partners))

    sent = []

    def send(src, dst, sems, to):
        c = pltpu.make_async_remote_copy(
            src_ref=src, dst_ref=dst, send_sem=sems.at[0], recv_sem=sems.at[1],
            device_id=to, device_id_type=MESH,
        )
        c.start()
        sent.append(c)
        return c

    loads[3].wait()
    over_z = [send(gathered.at[pos], gathered.at[pos], gz.at[d - 1], z_peer(d)) for d in (1, 2, 3)]

    loads[0].wait()

    @pl.loop(0, 16)
    def _(i):
        r = rows_at(i * 128, 128, 128)
        w_gu[r, 0:H] = (raw_g[r, :].astype(F32) * gate_s[...]).astype(BF)
        w_gu[r, H:HP] = jnp.zeros((128, HP - H), BF)

    for c in over_z:
        c.wait_recv()

    unit_a = gathered.at[pl.ds((y * 4 + x) * 2, 2)]
    unit_b = gathered.at[pl.ds(32 + (x * 4 + y) * 2, 2)]
    second = []
    for d in (1, 3, 2):
        second.append(send(unit_a, unit_a, gp.at[0, d - 1], x_peer(d)))
        second.append(send(unit_b, unit_b, gp.at[1, d - 1], y_peer(d)))

    loads[1].wait()

    @pl.loop(0, 16)
    def _(i):
        r = rows_at(i * 128, 128, 128)
        w_gu[r, HP:HP + H] = (raw_u[r, :].astype(F32) * up_s[...]).astype(BF)
        w_gu[r, HP + H:] = jnp.zeros((128, HP - H), BF)

    for c in second:
        c.wait_recv()

    line_a = gathered.at[pl.ds(y * 8, 8)]
    line_b = gathered.at[pl.ds(32 + x * 8, 8)]
    third = []
    for i, d in enumerate((1, 3)):
        third.append(
            (
                send(line_a, line_a, gn.at[0, i], y_peer(d)),
                send(line_b, line_b, gn.at[1, i], x_peer(d)),
            )
        )

    loads[2].wait()

    @pl.loop(0, 7)
    def _(i):
        r = rows_at(i * 64, 64, 64)
        w_d[r, :] = (raw_d[r, :].astype(F32) * down_s[r, :]).astype(BF)

    w_d[H:HP, :] = jnp.zeros((HP - H, D), BF)

    def repack(k):
        ahead = (0, 3, 1, 2)[k]
        for line, row in (((y + ahead) % 4 * 8, 0), (32 + (x + ahead) % 4 * 8, 64)):

            @pl.loop(0, 4)
            def _(j):
                a = gathered[line + 2 * j].astype(F32)
                b = gathered[line + 2 * j + 1].astype(F32)
                r = rows_at(k * 128 + row + j * 16, 16, 16)
                act[r, :] = jnp.concatenate([a[:8], b[:8]], axis=0).astype(BF)
                grad[r, :] = jnp.concatenate([a[8:], b[8:]], axis=0).astype(BF)

    def partials(k):
        r = pl.ds(k * 128, 128)

        @pl.loop(0, 4)
        def _(j):
            c = rows_at(j * 256, 256, 256)
            part[k, :, c] = jnp.dot(act[r, :], w_gu[:, c], preferred_element_type=F32)

        @pl.loop(0, 2)
        def _(j):
            c = rows_at(j * 256, 256, 256)
            part[k, :, rows_at(2 * HP + j * 256, 256, 256)] = contract_cols(grad[r, :], w_d[c, :])

        other = rows_at((1 - core) * 64, 64, 64)
        return send(part.at[k, other], sib.at[k], sc.at[k], sibling)

    def to_far(k, arrived):
        arrived.wait_recv()
        mine = rows_at(core * 64, 64, 64)
        s = part[k, mine, :] + sib[k]
        total[k] = s
        z_out[k] = s.astype(BF)
        return send(z_out.at[k], z_in.at[k], sz.at[k], far)

    def activate(k, arrived):
        arrived.wait_recv()
        gate_sum, up_sum, hidden_grad = (
            total[k, :, i * HP:(i + 1) * HP] + z_in[k, :, i * HP:(i + 1) * HP].astype(F32)
            for i in range(3)
        )
        gate_sigmoid = jax.nn.sigmoid(gate_sum)
        mine = rows_at(k * 128 + core * 64, 64, 64)
        hidden[mine, :] = (gate_sum * gate_sigmoid * up_sum).astype(BF)
        delta[mine, 0:HP] = (
            hidden_grad * up_sum * gate_sigmoid * (1.0 + gate_sum * (1.0 - gate_sigmoid))
        ).astype(BF)
        delta[mine, HP:] = (hidden_grad * gate_sum * gate_sigmoid).astype(BF)
        return [
            send(delta.at[mine], delta.at[mine], sd.at[0, k], sibling),
            send(hidden.at[mine], hidden.at[mine], sd.at[1, k], sibling),
        ]

    def input_part(k, arrived):
        arrived[0].wait_recv()
        r = pl.ds(k * 128, 128)

        @pl.loop(0, 8)
        def _(j):
            c = rows_at(j * 256, 256, 256)
            value = contract_cols(delta[r, :], w_gu[c, :])
            if k == 0:
                pi_own[:, c] = value
            else:
                pi_out[k - 1, :, c] = value.astype(BF)

        if k == 0:
            return []
        d = (0, 3, 1, 2)[k]
        return [
            send(pi_out.at[k - 1, 0:64], r1_in.at[0, k - 1], s1.at[0, k - 1], y_peer(d)),
            send(pi_out.at[k - 1, 64:128], r1_in.at[1, k - 1], s1.at[1, k - 1], x_peer(d)),
        ]

    repack(0)
    core_copy = [partials(0)]
    far_copy = [to_far(0, core_copy[0])]

    for c in third[0]:
        c.wait_recv()
    fwd_a = gathered.at[pl.ds((y + 3) % 4 * 8, 4)]
    fwd_b = gathered.at[pl.ds(32 + (x + 3) % 4 * 8, 4)]
    fourth = [
        send(fwd_a, fwd_a, gf.at[0, 0], y_peer(1)),
        send(fwd_b, fwd_b, gf.at[1, 0], x_peer(1)),
    ]
    for c in third[1]:
        c.wait_recv()
    back_a = gathered.at[pl.ds((y + 1) % 4 * 8 + 4, 4)]
    back_b = gathered.at[pl.ds(32 + (x + 1) % 4 * 8 + 4, 4)]
    fourth += [
        send(back_a, back_a, gf.at[0, 1], y_peer(3)),
        send(back_b, back_b, gf.at[1, 1], x_peer(3)),
    ]
    repack(1)
    core_copy.append(partials(1))
    repack(2)
    far_copy.append(to_far(1, core_copy[1]))
    core_copy.append(partials(2))
    far_copy.append(to_far(2, core_copy[2]))
    for c in fourth:
        c.wait_recv()
    repack(3)
    core_copy.append(partials(3))
    far_copy.append(to_far(3, core_copy[3]))

    over_1 = []
    deltas = []
    for k in range(4):
        deltas.append(activate(k, far_copy[k]))
        over_1 += input_part(k, deltas[k])

    for c in over_1:
        c.wait_recv()
    over_2 = []
    for i, me in ((0, x), (1, y)):
        own = pi_own[i * 64:i * 64 + 64, :]
        for k in range(3):
            own = own + r1_in[i, k].astype(F32)
        r2_own[i] = own
        r2_out[i] = own.astype(BF)
        peer = (x_peer, y_peer)[i]
        for d in (2, 1, 3):
            to = rows_at((me + d) % 4 * 16, 16, 16)
            over_2.append(send(r2_out.at[i, to], r2_in.at[i, d - 1], s2.at[i, d - 1], peer(d)))
    for c in over_2:
        c.wait_recv()
    for i, me in ((0, x), (1, y)):
        own = r2_own[i, rows_at(me * 16, 16, 16), :]
        for d in range(3):
            own = own + r2_in[i, d].astype(F32)
        for j in range(2):
            own_j = own[j * 8:j * 8 + 8]
            r3_own[2 * i + j] = own_j
            r3_out[2 * i + j] = jnp.concatenate([own_j[:, :1024], own_j[:, 1024:]], axis=0).astype(BF)
    over_3 = []
    for d in (2, 1, 3):
        over_3.append(send(r3_out.at[(z + d) % 4], r3_in.at[d - 1], s3.at[d - 1], z_peer(d)))
    for c in over_3:
        c.wait_recv()
    own = r3_own[z]
    for d in range(3):
        got = r3_in[d].astype(F32)
        own = own + jnp.concatenate([got[:8], got[8:]], axis=1)
    dx[...] = own

    for pair in deltas:
        pair[1].wait_recv()
    for c in sent:
        c.wait_send()


def local(
    quant_input, input_scale, grad_output, gate_quant, gate_scale, up_quant, up_scale, down_quant, down_scale,
):
    activations = (quant_input.astype(F32) * input_scale[:, None]).astype(BF)
    slab = jnp.concatenate([activations, grad_output], axis=0)
    vmem = pl.BlockSpec(memory_space=pltpu.VMEM)
    hbm = pl.BlockSpec(memory_space=pl.ANY)
    dma = pltpu.SemaphoreType.DMA
    dx, act, grad, delta, hidden = pl.pallas_call(
        kernel,
        name="ffn_backward",
        out_shape=(
            jax.ShapeDtypeStruct((8, D), F32),
            jax.ShapeDtypeStruct((TOKENS, D), BF),
            jax.ShapeDtypeStruct((TOKENS, D), BF),
            jax.ShapeDtypeStruct((TOKENS, 2 * HP), BF),
            jax.ShapeDtypeStruct((TOKENS, HP), BF),
        ),
        in_specs=[vmem, hbm, hbm, hbm, vmem, vmem, vmem],
        out_specs=(vmem,) * 5,
        scratch_shapes=[
            pltpu.VMEM((64, 16, D), BF),
            pltpu.VMEM((D, H), BF),
            pltpu.VMEM((D, H), BF),
            pltpu.VMEM((H, D), BF),
            pltpu.VMEM((D, 2 * HP), BF),
            pltpu.VMEM((HP, D), BF),
            pltpu.VMEM((4, 128, 3 * HP), F32),
            pltpu.VMEM((4, 64, 3 * HP), F32),
            pltpu.VMEM((4, 64, 3 * HP), F32),
            pltpu.VMEM((4, 64, 3 * HP), BF),
            pltpu.VMEM((4, 64, 3 * HP), BF),
            pltpu.VMEM((128, D), F32),
            pltpu.VMEM((3, 128, D), BF),
            pltpu.VMEM((2, 3, 64, D), BF),
            pltpu.VMEM((2, 64, D), F32),
            pltpu.VMEM((2, 64, D), BF),
            pltpu.VMEM((2, 3, 16, D), BF),
            pltpu.VMEM((4, 8, D), F32),
            pltpu.VMEM((4, 16, D // 2), BF),
            pltpu.VMEM((3, 16, D // 2), BF),
            dma((4,)),
            dma((3, 2)),
            dma((2, 3, 2)),
            dma((2, 2, 2)),
            dma((2, 2, 2)),
            dma((4, 2)),
            dma((4, 2)),
            dma((2, 4, 2)),
            dma((2, 3, 2)),
            dma((2, 3, 2)),
            dma((3, 2)),
        ],
        compiler_params=pltpu.CompilerParams(
            collective_id=0, has_side_effects=True, vmem_limit_bytes=48 * 2**20
        ),
        cost_estimate=pl.CostEstimate(flops=6 * 10**9, bytes_accessed=12 * 10**6, transcendentals=300000),
    )(
        slab, gate_quant, up_quant, down_quant,
        gate_scale.reshape(1, H), up_scale.reshape(1, H), down_scale.reshape(H, 1),
    )
    gate_grad = contract_rows(act, delta[:, :H]).astype(BF)
    up_grad = contract_rows(act, delta[:, HP:HP + H]).astype(BF)
    down_grad = contract_rows(hidden[:, :H], grad).astype(BF)
    return (dx.astype(BF), gate_grad, up_grad, down_grad)


def solution(mesh):
    in_specs = (
        P("hid", "mdl"),
        P("hid"),
        P("hid", "mdl"),
        P("mdl", "hid"),
        P("hid"),
        P("mdl", "hid"),
        P("hid"),
        P("hid", "mdl"),
        P("hid"),
    )
    out_specs = (P("hid", "mdl"), P("mdl", "hid"), P("mdl", "hid"), P("hid", "mdl"))
    return jax.shard_map(local, mesh=mesh, in_specs=in_specs, out_specs=out_specs, check_vma=False)
```

```python
import jax
import jax.numpy as jnp
from jax import lax
from jax.experimental import pallas as pl
from jax.experimental.pallas import tpu as pltpu
from jax.sharding import PartitionSpec as P

MESH = pl.DeviceIdType.MESH
BF = jnp.bfloat16
F32 = jnp.float32
D = 2048
H = 448
HP = 512
TOKENS = 512
PIECES = ((0, 64), (64, 64), (128, 128), (256, 128), (384, 128))
GROUPS = {
    2: ((3, 0, 4), (1, 4, 4)),
    3: ((2, 0, 8),),
    4: ((3, 4, 4), (1, 0, 4)),
}


def contract_cols(left, right):
    return lax.dot_general(left, right, (((1,), (1,)), ((), ())), preferred_element_type=F32)


def rows_at(start, size, step):
    return pl.ds(pl.multiple_of(start, step), size)


def packed(s):
    last = s[:, 384:512] + pltpu.roll(s[:, 896:1024], 64, 1)
    return jnp.concatenate([s[:, 0:384], s[:, 512:896], s[:, 1024:1408], last, s[:, 1408:1536]], axis=1)


def unpacked(p):
    shared = p[:, 1152:1280]
    low = lax.broadcasted_iota(jnp.int32, shared.shape, 1) < 64
    gate = jnp.where(low, shared, 0.0)
    up = jnp.where(low, pltpu.roll(shared, 64, 1), 0.0)
    return (
        jnp.concatenate([p[:, 0:384], gate], axis=1),
        jnp.concatenate([p[:, 384:768], up], axis=1),
        jnp.concatenate([p[:, 768:1152], p[:, 1280:1408]], axis=1),
    )


def kernel(
    quant, scale, cotangent, gate_q, up_q, down_q, gate_s, up_s, down_s,
    dx, gate_grad, up_grad, down_grad,
    mine_q, mine_g, mine_s, scale_rows, scales, gathered, raw, act, grad, delta, turned, w_gu, w_d, part, sib, total, z_out, z_in,
    pi_own, pi_out, r1_in, r2_own, r2_out, r2_in, r3_own, r3_out, r3_in,
    load_sem, gz, gp, gn, gf, sc, sz, sd, s1, s2, s3,
):
    hid = lax.axis_index("hid")
    mdl = lax.axis_index("mdl")
    x, z, y = hid % 4, (hid // 4) % 4, hid // 16
    core, half = mdl % 2, mdl // 2
    kinds = (z // 2, 1 - z // 2)

    def at(px, py, pz):
        return (py * 4 + pz) * 4 + px

    def near_peer(role, d):
        k = kinds[role]
        return (at((x + d * (1 - k)) % 4, (y + d * k) % 4, z), mdl)

    def line_peer(role, d):
        k = kinds[role]
        return (at((x + d * k) % 4, (y + d * (1 - k)) % 4, z), mdl)

    planes = (z, z + 1 - 2 * (z % 2), (z + 2) % 4, 3 - z)
    sibling = (hid, half * 2 + (1 - core))
    far = (hid, (1 - half) * 2 + core)

    def place(pz):
        k = pz // 2
        return k * 32 + ((y * 4 + x) * (1 - k) + (x * 4 + y) * k) * 2 + pz % 2

    def line_start(role, ahead):
        k = kinds[role]
        return k * 32 + ((y * (1 - k) + x * k) + ahead) % 4 * 8

    def line(role, ahead, first, size):
        return gathered.at[pl.ds(line_start(role, ahead) + first, size)]

    loads = [
        pltpu.make_async_copy(src, dst, load_sem.at[i])
        for i, (src, dst) in enumerate(
            [(gate_q, raw.at[0]), (up_q, raw.at[1]), (down_q, raw.at[2]), (quant, mine_q), (cotangent, mine_g)]
            + [(scale, mine_s)]
            + [(s, scale_rows.at[i]) for i, s in enumerate((gate_s, up_s, down_s))]
        )
    ]
    for i in (5, 3, 4, 6, 7, 8, 2, 0, 1):
        loads[i].start()

    barrier = pltpu.get_barrier_semaphore()
    partners = [f(0, d) for f in (near_peer, line_peer) for d in (1, 2, 3)]
    partners += [(at(x, y, p), mdl) for p in planes[1:]] + [sibling, far]
    for p in partners:
        pl.semaphore_signal(barrier, inc=1, device_id=p, device_id_type=MESH)

    pos = place(z)
    for i in range(3, 9):
        loads[i].wait()
    row = lax.broadcasted_iota(jnp.int32, (8, 1), 0)
    factor = jnp.zeros((8, 1), F32)
    for i in range(8):
        factor = jnp.where(row == i, mine_s[i], factor)
    gathered[pos] = jnp.concatenate(
        [mine_q[...].astype(F32) * factor, mine_g[...].astype(F32)], axis=0
    ).astype(BF)
    for i in range(3):
        scales[:, 8 * i:8 * i + 8] = jnp.broadcast_to(scale_rows[i], (8, H)).T

    pl.semaphore_wait(barrier, len(partners))

    sent = []

    def send(src, dst, sems, to):
        c = pltpu.make_async_remote_copy(
            src_ref=src, dst_ref=dst, send_sem=sems.at[0], recv_sem=sems.at[1],
            device_id=to, device_id_type=MESH,
        )
        c.start()
        sent.append(c)
        return c

    second = {}

    def over_near(b):
        block = gathered.at[place(planes[b])]
        second[b] = [send(block, block, gp.at[b, e - 1], near_peer(b // 2, e)) for e in (1, 3, 2)]

    own_slab = gathered.at[pos]
    over_z = {b: send(own_slab, own_slab, gz.at[b - 1], (at(x, y, planes[b]), mdl)) for b in (1, 2, 3)}
    over_near(0)

    def dequantize(i, out, row):
        loads[i].wait()

        @pl.loop(0, 7)
        def _(j):
            r = rows_at(j * 64, 64, 64)
            out[rows_at(row + j * 64, 64, 64), :] = (
                raw[i, r, :].astype(F32) * scales[r, 8 * i:8 * i + 1]
            ).astype(BF)

        out[row + H:row + HP, :] = jnp.zeros((HP - H, D), BF)

    dequantize(2, w_d, 0)
    over_z[1].wait_recv()
    over_near(1)
    dequantize(0, w_gu, 0)
    for b in (3, 2):
        over_z[b].wait_recv()
        over_near(b)
    dequantize(1, w_gu, HP)

    def own_line(role, step):
        out = []
        for i, d in enumerate((1, 3)):
            block = line(role, 0, 4 * (step ^ i), 4)
            out.append(send(block, block, gn.at[step, role, i], line_peer(role, d)))
        return out

    def pass_on(role, arrived):
        for c in arrived:
            c.wait_recv()
        out = []
        for i, d in enumerate((1, 3)):
            block = line(role, 4 - d, 4 * i, 4)
            out.append(send(block, block, gf.at[role, i], line_peer(role, d)))
        return out

    def repack(p):
        start, size = PIECES[p]
        jobs = [(p, 0, 0, 8)] if p < 2 else [(o,) + g for o in range(2) for g in GROUPS[p]]
        for role, ahead, first, n in jobs:
            base = line_start(role, ahead) + first

            @pl.loop(0, n // 2)
            def _(j):
                a = gathered[base + 2 * j].astype(F32)
                b = gathered[base + 2 * j + 1].astype(F32)
                r = rows_at(start + j * 16, 16, 16)
                act[r, :] = jnp.concatenate([a[:8], b[:8]], axis=0).astype(BF)
                grad[r, :] = jnp.concatenate([a[8:], b[8:]], axis=0).astype(BF)

            start += n * 8

    def own_rows(p):
        start, size = PIECES[p]
        return rows_at(start + core * (size // 2), size // 2, 32)

    def sums_rows(p):
        return pl.ds(PIECES[p][0] // 2, PIECES[p][1] // 2)

    def partials(p):
        repack(p)
        start, size = PIECES[p]
        r = pl.ds(start, size)

        @pl.loop(0, 4)
        def _(j):
            c = rows_at(j * 256, 256, 256)
            part[r, c] = contract_cols(act[r, :], w_gu[c, :])

        @pl.loop(0, 2)
        def _(j):
            c = rows_at(j * 256, 256, 256)
            part[r, rows_at(2 * HP + j * 256, 256, 256)] = contract_cols(grad[r, :], w_d[c, :])

        other = rows_at(start + (1 - core) * (size // 2), size // 2, 32)
        return send(part.at[other], sib.at[sums_rows(p)], sc.at[p], sibling)

    def to_far(p, arrived):
        arrived.wait_recv()
        r = sums_rows(p)
        s = part[own_rows(p), :] + sib[r, :]
        total[r, :] = s
        z_out[r, :] = packed(s).astype(BF)
        return send(z_out.at[r], z_in.at[r], sz.at[p], far)

    def activate(p, arrived):
        arrived.wait_recv()
        r = sums_rows(p)
        gate_sum, up_sum, hidden_grad = (
            total[r, i * HP:(i + 1) * HP] + v for i, v in enumerate(unpacked(z_in[r, :].astype(F32)))
        )
        gate_sigmoid = jax.nn.sigmoid(gate_sum)
        mine = own_rows(p)
        delta[mine, 0:HP] = (
            hidden_grad * up_sum * gate_sigmoid * (1.0 + gate_sum * (1.0 - gate_sigmoid))
        ).astype(BF)
        delta[mine, HP:2 * HP] = (hidden_grad * gate_sum * gate_sigmoid).astype(BF)
        delta[mine, 2 * HP:] = (gate_sum * gate_sigmoid * up_sum).astype(BF)
        return send(delta.at[mine], delta.at[mine], sd.at[p], sibling)

    over_1 = []

    def input_part(k, arrived):
        for c in arrived:
            c.wait_recv()
        r = pl.ds(k * 128, 128)

        @pl.loop(0, 8)
        def _(j):
            c = rows_at(j * 256, 256, 256)
            value = jnp.dot(delta[r, 0:2 * HP], w_gu[:, c], preferred_element_type=F32)
            if k == 0:
                pi_own[:, c] = value
            else:
                pi_out[k - 1, :, c] = value.astype(BF)

        if k > 0:
            row = 0
            for role in range(2):
                for i, (ahead, first, size) in enumerate(GROUPS[k + 1]):
                    n = size * 8
                    over_1.append(
                        send(
                            pi_out.at[k - 1, row:row + n],
                            r1_in.at[role, {3: 0, 1: 1, 2: 2}[ahead], first * 8:first * 8 + n],
                            s1.at[k - 1, role, i],
                            line_peer(role, ahead),
                        )
                    )
                    row += n

    def turn(k):
        r = pl.ds(k * 128, 128)
        for i in range(12):
            turned[i * 128:(i + 1) * 128, r] = delta[r, i * 128:(i + 1) * 128].T

    def weight_grad(i, tokens, out):
        @pl.loop(0, 8)
        def _(j):
            c = rows_at(j * 256, 256, 256)
            out[:, c] = jnp.dot(
                turned[i * HP:i * HP + H, :], tokens[:, c], preferred_element_type=F32
            ).astype(BF)

    core_copy, far_copy, ready = {}, {}, {}
    third = {}
    for c in second[0] + second[1]:
        c.wait_recv()
    third[0, 0] = own_line(0, 0)
    core_copy[0] = partials(0)
    for c in second[2] + second[3]:
        c.wait_recv()
    third[1, 0] = own_line(1, 0)
    far_copy[0] = to_far(0, core_copy[0])
    core_copy[1] = partials(1)
    fourth = pass_on(0, third[0, 0])
    far_copy[1] = to_far(1, core_copy[1])
    fourth += pass_on(1, third[1, 0])
    core_copy[2] = partials(2)
    third[0, 1] = own_line(0, 1)
    third[1, 1] = own_line(1, 1)
    ready[0] = activate(0, far_copy[0])
    far_copy[2] = to_far(2, core_copy[2])
    for c in fourth:
        c.wait_recv()
    core_copy[3] = partials(3)
    ready[1] = activate(1, far_copy[1])
    far_copy[3] = to_far(3, core_copy[3])
    input_part(0, [ready[0], ready[1]])
    for c in third[0, 1] + third[1, 1]:
        c.wait_recv()
    core_copy[4] = partials(4)
    turn(0)
    far_copy[4] = to_far(4, core_copy[4])
    for k in (1, 2, 3):
        ready[k + 1] = activate(k + 1, far_copy[k + 1])
        input_part(k, [ready[k + 1]])
        turn(k)

    weight_grad(0, act, gate_grad)
    for c in over_1:
        c.wait_recv()
    over_2 = []
    for role in range(2):
        own = pi_own[role * 64:role * 64 + 64, :]
        for k in range(3):
            own = own + r1_in[role, k].astype(F32)
        r2_own[role] = own
        r2_out[role] = own.astype(BF)
        k = kinds[role]
        me = x * (1 - k) + y * k
        for d in (2, 1, 3):
            to = rows_at((me + d) % 4 * 16, 16, 16)
            over_2.append(send(r2_out.at[role, to], r2_in.at[role, d - 1], s2.at[role, d - 1], near_peer(role, d)))
    weight_grad(1, act, up_grad)
    for c in over_2:
        c.wait_recv()
    for role in range(2):
        k = kinds[role]
        me = x * (1 - k) + y * k
        own = r2_own[role, rows_at(me * 16, 16, 16), :]
        for d in range(3):
            own = own + r2_in[role, d].astype(F32)
        for j in range(2):
            own_j = own[j * 8:j * 8 + 8]
            r3_own[2 * k + j] = own_j
            r3_out[2 * k + j] = jnp.concatenate([own_j[:, :1024], own_j[:, 1024:]], axis=0).astype(BF)
    over_3 = []
    for b in (2, 3, 1):
        over_3.append(send(r3_out.at[planes[b]], r3_in.at[b - 1], s3.at[b - 1], (at(x, y, planes[b]), mdl)))
    weight_grad(2, grad, down_grad)
    for c in over_3:
        c.wait_recv()
    own = r3_own[z]
    for d in range(3):
        got = r3_in[d].astype(F32)
        own = own + jnp.concatenate([got[:8], got[8:]], axis=1)
    dx[...] = own

    for c in sent:
        c.wait_send()


def store(dx, gate_grad, up_grad, down_grad, dx_out, gate_out, up_out, down_out, rounded, sem):
    copies = [
        pltpu.make_async_copy(src, dst, sem.at[i])
        for i, (src, dst) in enumerate([(gate_grad, gate_out), (up_grad, up_out), (down_grad, down_out)])
    ]
    for c in copies:
        c.start()
    rounded[...] = dx[...].astype(BF)
    copies.append(pltpu.make_async_copy(rounded, dx_out, sem.at[3]))
    copies[3].start()
    for c in copies:
        c.wait()


def local(
    quant_input, input_scale, grad_output, gate_quant, gate_scale, up_quant, up_scale, down_quant, down_scale,
):
    vmem = pl.BlockSpec(memory_space=pltpu.VMEM)
    hbm = pl.BlockSpec(memory_space=pltpu.HBM)
    dma = pltpu.SemaphoreType.DMA
    weight = jax.ShapeDtypeStruct((H, D), BF)
    dx, gate_grad, up_grad, down_grad = pl.pallas_call(
        kernel,
        name="ffn_backward",
        out_shape=(jax.ShapeDtypeStruct((8, D), F32), weight, weight, weight),
        in_specs=[hbm] * 9,
        out_specs=(vmem,) * 4,
        scratch_shapes=[
            pltpu.VMEM((8, D), BF),
            pltpu.VMEM((8, D), BF),
            pltpu.SMEM((8,), F32),
            pltpu.VMEM((3, 1, H), F32),
            pltpu.VMEM((H, 24), F32),
            pltpu.VMEM((64, 16, D), BF),
            pltpu.VMEM((3, H, D), BF),
            pltpu.VMEM((TOKENS, D), BF),
            pltpu.VMEM((TOKENS, D), BF),
            pltpu.VMEM((TOKENS, 3 * HP), BF),
            pltpu.VMEM((3 * HP, TOKENS), BF),
            pltpu.VMEM((2 * HP, D), BF),
            pltpu.VMEM((HP, D), BF),
            pltpu.VMEM((TOKENS, 3 * HP), F32),
            pltpu.VMEM((TOKENS // 2, 3 * HP), F32),
            pltpu.VMEM((TOKENS // 2, 3 * HP), F32),
            pltpu.VMEM((TOKENS // 2, 11 * 128), BF),
            pltpu.VMEM((TOKENS // 2, 11 * 128), BF),
            pltpu.VMEM((128, D), F32),
            pltpu.VMEM((3, 128, D), BF),
            pltpu.VMEM((2, 3, 64, D), BF),
            pltpu.VMEM((2, 64, D), F32),
            pltpu.VMEM((2, 64, D), BF),
            pltpu.VMEM((2, 3, 16, D), BF),
            pltpu.VMEM((4, 8, D), F32),
            pltpu.VMEM((4, 16, D // 2), BF),
            pltpu.VMEM((3, 16, D // 2), BF),
            dma((9,)),
            dma((3, 2)),
            dma((4, 3, 2)),
            dma((2, 2, 2, 2)),
            dma((2, 2, 2)),
            dma((5, 2)),
            dma((5, 2)),
            dma((5, 2)),
            dma((3, 2, 2, 2)),
            dma((2, 3, 2)),
            dma((3, 2)),
        ],
        compiler_params=pltpu.CompilerParams(
            collective_id=0, has_side_effects=True, vmem_limit_bytes=40 * 2**20
        ),
        cost_estimate=pl.CostEstimate(flops=9 * 10**9, bytes_accessed=12 * 10**6, transcendentals=300000),
    )(
        *(
            pltpu.with_memory_space_constraint(a, pltpu.HBM)
            for a in (
                quant_input, input_scale, grad_output, gate_quant.T, up_quant.T, down_quant,
                gate_scale.reshape(1, H), up_scale.reshape(1, H), down_scale.reshape(1, H),
            )
        )
    )
    dx, gate_grad, up_grad, down_grad = pl.pallas_call(
        store,
        name="store",
        out_shape=(pltpu.HBM((8, D), BF),) + (pltpu.HBM((H, D), BF),) * 3,
        in_specs=[vmem] * 4,
        out_specs=(hbm,) * 4,
        scratch_shapes=[pltpu.VMEM((8, D), BF), dma((4,))],
        compiler_params=pltpu.CompilerParams(vmem_limit_bytes=2**20),
    )(*(pltpu.with_memory_space_constraint(a, pltpu.VMEM) for a in (dx, gate_grad, up_grad, down_grad)))
    return (dx, gate_grad.T, up_grad.T, down_grad)


def solution(mesh):
    in_specs = (
        P("hid", "mdl"),
        P("hid"),
        P("hid", "mdl"),
        P("mdl", "hid"),
        P("hid"),
        P("mdl", "hid"),
        P("hid"),
        P("hid", "mdl"),
        P("hid"),
    )
    out_specs = (P("hid", "mdl"), P("mdl", "hid"), P("mdl", "hid"), P("hid", "mdl"))
    return jax.shard_map(local, mesh=mesh, in_specs=in_specs, out_specs=out_specs, check_vma=False)
```

```python
import jax
import jax.numpy as jnp
from jax import lax
from jax.experimental import pallas as pl
from jax.experimental.pallas import tpu as pltpu
from jax.sharding import PartitionSpec as P

MESH = pl.DeviceIdType.MESH
BF = jnp.bfloat16
F32 = jnp.float32
D = 2048
H = 448
HP = 512
TOKENS = 512
STEP = 64
PARTS = 2
PART = D // PARTS
GROUPS = (
    ((0, 0, 8),),
    ((3, 0, 4), (1, 4, 4)),
    ((2, 0, 8),),
    ((3, 4, 4), (1, 0, 4)),
)


def contract_cols(left, right):
    return lax.dot_general(left, right, (((1,), (1,)), ((), ())), preferred_element_type=F32)


def rows_at(start, size, step):
    return pl.ds(pl.multiple_of(start, step), size)


def packed(s):
    last = s[:, 384:512] + pltpu.roll(s[:, 896:1024], 64, 1)
    return jnp.concatenate([s[:, 0:384], s[:, 512:896], s[:, 1024:1408], last, s[:, 1408:1536]], axis=1)


def unpacked(p):
    shared = p[:, 1152:1280]
    low = lax.broadcasted_iota(jnp.int32, shared.shape, 1) < 64
    gate = jnp.where(low, shared, 0.0)
    up = jnp.where(low, pltpu.roll(shared, 64, 1), 0.0)
    return (
        jnp.concatenate([p[:, 0:384], gate], axis=1),
        jnp.concatenate([p[:, 384:768], up], axis=1),
        jnp.concatenate([p[:, 768:1152], p[:, 1280:1408]], axis=1),
    )


def kernel(
    quant, scale, cotangent, gate_q, up_q, down_q, gate_s, up_s, down_s,
    dx, gate_grad, up_grad, down_grad,
    mine_q, mine_g, mine_s, scale_rows, scales, gathered, raw, act, grad, delta, turned, w_gu, w_d, part, sib, total, z_out, z_in,
    pi_own, pi_out, r1_in, r2_own, r2_out, r2_in, r3_own, r3_out, r3_in,
    load_sem, gz, gp, gn, gf, sc, sz, sd, s1, s2, s3,
):
    hid = lax.axis_index("hid")
    mdl = lax.axis_index("mdl")
    x, z, y = hid % 4, (hid // 4) % 4, hid // 16
    core, half = mdl % 2, mdl // 2
    kinds = (z // 2, 1 - z // 2)

    def at(px, py, pz):
        return (py * 4 + pz) * 4 + px

    def near_peer(role, d):
        k = kinds[role]
        return (at((x + d * (1 - k)) % 4, (y + d * k) % 4, z), mdl)

    def line_peer(role, d):
        k = kinds[role]
        return (at((x + d * k) % 4, (y + d * (1 - k)) % 4, z), mdl)

    planes = (z, z + 1 - 2 * (z % 2), (z + 2) % 4, 3 - z)
    sibling = (hid, half * 2 + (1 - core))
    far = (hid, (1 - half) * 2 + core)

    def place(pz):
        k = pz // 2
        return k * 32 + ((y * 4 + x) * (1 - k) + (x * 4 + y) * k) * 2 + pz % 2

    def line_start(role, ahead):
        k = kinds[role]
        return k * 32 + ((y * (1 - k) + x * k) + ahead) % 4 * 8

    def line(role, ahead, first, size):
        return gathered.at[pl.ds(line_start(role, ahead) + first, size)]

    loads = [
        pltpu.make_async_copy(src, dst, load_sem.at[i])
        for i, (src, dst) in enumerate(
            [(gate_q, raw.at[0]), (up_q, raw.at[1]), (down_q, raw.at[2]), (quant, mine_q), (cotangent, mine_g)]
            + [(scale, mine_s)]
            + [(s, scale_rows.at[i]) for i, s in enumerate((gate_s, up_s, down_s))]
        )
    ]
    for i in (5, 3, 4, 6, 7, 8, 2, 0, 1):
        loads[i].start()

    barrier = pltpu.get_barrier_semaphore()
    partners = [f(0, d) for f in (near_peer, line_peer) for d in (1, 2, 3)]
    partners += [(at(x, y, p), mdl) for p in planes[1:]] + [sibling, far]
    for p in partners:
        pl.semaphore_signal(barrier, inc=1, device_id=p, device_id_type=MESH)

    pos = place(z)
    for i in range(3, 9):
        loads[i].wait()
    row = lax.broadcasted_iota(jnp.int32, (8, 1), 0)
    factor = jnp.zeros((8, 1), F32)
    for i in range(8):
        factor = jnp.where(row == i, mine_s[i], factor)
    gathered[pos] = jnp.concatenate(
        [mine_q[...].astype(F32) * factor, mine_g[...].astype(F32)], axis=0
    ).astype(BF)
    for i in range(3):
        scales[:, 8 * i:8 * i + 8] = jnp.broadcast_to(scale_rows[i], (8, H)).T

    pl.semaphore_wait(barrier, len(partners))

    sent = []

    def send(src, dst, sems, to):
        c = pltpu.make_async_remote_copy(
            src_ref=src, dst_ref=dst, send_sem=sems.at[0], recv_sem=sems.at[1],
            device_id=to, device_id_type=MESH,
        )
        c.start()
        sent.append(c)
        return c

    second = {}

    def over_near(b):
        block = gathered.at[place(planes[b])]
        second[b] = [send(block, block, gp.at[b, e - 1], near_peer(b // 2, e)) for e in (1, 3, 2)]

    over_z = {}

    def to_plane(b):
        own_slab = gathered.at[pos]
        over_z[b] = send(own_slab, own_slab, gz.at[b - 1], (at(x, y, planes[b]), mdl))

    to_plane(1)
    over_near(0)

    def dequantize(i, out, row):
        loads[i].wait()

        @pl.loop(0, 7)
        def _(j):
            r = rows_at(j * 64, 64, 64)
            out[rows_at(row + j * 64, 64, 64), :] = (
                raw[i, r, :].astype(F32) * scales[r, 8 * i:8 * i + 1]
            ).astype(BF)

        out[row + H:row + HP, :] = jnp.zeros((HP - H, D), BF)

    dequantize(2, w_d, 0)
    to_plane(3)
    to_plane(2)
    over_z[1].wait_recv()
    over_near(1)
    dequantize(0, w_gu, 0)
    for b in (3, 2):
        over_z[b].wait_recv()
        over_near(b)
    dequantize(1, w_gu, HP)

    def own_line(role, step):
        out = []
        for i, d in enumerate((1, 3)):
            block = line(role, 0, 4 * (step ^ i), 4)
            out.append(send(block, block, gn.at[step, role, i], line_peer(role, d)))
        return out

    def pass_on(role, arrived):
        for c in arrived:
            c.wait_recv()
        out = []
        for i, d in enumerate((1, 3)):
            block = line(role, 4 - d, 4 * i, 4)
            out.append(send(block, block, gf.at[role, i], line_peer(role, d)))
        return out

    def own_rows(p):
        return rows_at(p * STEP + core * (STEP // 2), STEP // 2, STEP // 2)

    def sums_rows(p):
        return pl.ds(p * (STEP // 2), STEP // 2)

    core_copy, far_copy, ready = {}, {}, {}

    def partials(p):
        start = p * STEP
        for ahead, first, n in GROUPS[p // 2]:
            base = line_start(p % 2, ahead) + first

            @pl.loop(0, n // 2)
            def _(j):
                a = gathered[base + 2 * j].astype(F32)
                b = gathered[base + 2 * j + 1].astype(F32)
                r = rows_at(start + j * 16, 16, 16)
                act[r, :] = jnp.concatenate([a[:8], b[:8]], axis=0).astype(BF)
                grad[r, :] = jnp.concatenate([a[8:], b[8:]], axis=0).astype(BF)

            start += n * 8
        r = pl.ds(p * STEP, STEP)

        @pl.loop(0, 1)
        def _(j):
            c = rows_at(j * 1024, 1024, 1024)
            part[r, c] = contract_cols(act[r, :], w_gu[c, :])

        @pl.loop(0, 1)
        def _(j):
            c = rows_at(j * 512, 512, 512)
            part[r, rows_at(2 * HP + j * 512, 512, 512)] = contract_cols(grad[r, :], w_d[c, :])

        other = rows_at(p * STEP + (1 - core) * (STEP // 2), STEP // 2, STEP // 2)
        core_copy[p] = send(part.at[other], sib.at[sums_rows(p)], sc.at[p], sibling)

    def to_far(p):
        core_copy[p].wait_recv()
        r = sums_rows(p)
        s = part[own_rows(p), :] + sib[r, :]
        total[r, :] = s
        z_out[r, :] = packed(s).astype(BF)
        far_copy[p] = send(z_out.at[r], z_in.at[r], sz.at[p], far)

    def activate(p):
        far_copy[p].wait_recv()
        r = sums_rows(p)
        gate_sum, up_sum, hidden_grad = (
            total[r, i * HP:(i + 1) * HP] + v for i, v in enumerate(unpacked(z_in[r, :].astype(F32)))
        )
        gate_sigmoid = jax.nn.sigmoid(gate_sum)
        mine = own_rows(p)
        delta[mine, 0:HP] = (
            hidden_grad * up_sum * gate_sigmoid * (1.0 + gate_sum * (1.0 - gate_sigmoid))
        ).astype(BF)
        delta[mine, HP:2 * HP] = (hidden_grad * gate_sum * gate_sigmoid).astype(BF)
        delta[mine, 2 * HP:] = (gate_sum * gate_sigmoid * up_sum).astype(BF)
        ready[p] = send(delta.at[mine], delta.at[mine], sd.at[p], sibling)

    over_1 = [[] for _ in range(PARTS)]

    def input_part(k):
        ready[2 * k].wait_recv()
        ready[2 * k + 1].wait_recv()
        r = pl.ds(k * 128, 128)
        for q in range(PARTS):

            @pl.loop(q * PART // 1024, (q + 1) * PART // 1024)
            def _(j):
                c = rows_at(j * 1024, 1024, 1024)
                value = jnp.dot(delta[r, 0:2 * HP], w_gu[:, c], preferred_element_type=F32)
                if k == 0:
                    pi_own[:, c] = value
                else:
                    pi_out[k - 1, :, c] = value.astype(BF)

            if k == 0:
                continue
            row = 0
            columns = slice(q * PART, (q + 1) * PART)
            for role in range(2):
                for i, (ahead, first, size) in enumerate(GROUPS[k]):
                    n = size * 8
                    over_1[q].append(
                        send(
                            pi_out.at[k - 1, row:row + n, columns],
                            r1_in.at[role, {3: 0, 1: 1, 2: 2}[ahead], first * 8:first * 8 + n, columns],
                            s1.at[q, k - 1, role, i],
                            line_peer(role, ahead),
                        )
                    )
                    row += n

    def turn(k):
        r = pl.ds(k * 128, 128)
        for i in range(12):
            turned[i * 128:(i + 1) * 128, r] = delta[r, i * 128:(i + 1) * 128].T

    def weight_grad(i, tokens, out):
        @pl.loop(0, 2)
        def _(j):
            c = rows_at(j * 1024, 1024, 1024)
            out[:, c] = jnp.dot(
                turned[i * HP:i * HP + H, :], tokens[:, c], preferred_element_type=F32
            ).astype(BF)

    third, fourth = {}, {}

    def arrive(copies):
        for c in copies:
            c.wait_recv()

    arrive(second[0] + second[1])
    third[0, 0] = own_line(0, 0)
    partials(0)
    arrive(second[2] + second[3])
    third[1, 0] = own_line(1, 0)
    to_far(0)
    partials(1)
    fourth[0] = pass_on(0, third[0, 0])
    third[0, 1] = own_line(0, 1)
    to_far(1)
    partials(2)
    fourth[1] = pass_on(1, third[1, 0])
    third[1, 1] = own_line(1, 1)
    to_far(2)
    partials(3)
    activate(0)
    to_far(3)
    activate(1)
    arrive(fourth[0])
    partials(4)
    input_part(0)
    to_far(4)
    arrive(fourth[1])
    partials(5)
    turn(0)
    to_far(5)
    arrive(third[0, 1])
    partials(6)
    activate(2)
    to_far(6)
    arrive(third[1, 1])
    partials(7)
    activate(3)
    to_far(7)
    input_part(1)
    turn(1)
    activate(4)
    activate(5)
    input_part(2)
    turn(2)
    activate(6)
    activate(7)
    input_part(3)
    turn(3)

    def own_place(role):
        k = kinds[role]
        return x * (1 - k) + y * k

    over_2, over_3 = {}, {}

    def to_near(q):
        for c in over_1[q]:
            c.wait_recv()
        columns = slice(q * PART, (q + 1) * PART)
        over_2[q] = []
        for role in range(2):
            own = pi_own[role * 64:role * 64 + 64, columns]
            for i in range(3):
                own = own + r1_in[role, i, :, columns].astype(F32)
            r2_own[role, :, columns] = own
            r2_out[role, :, columns] = own.astype(BF)
            for d in (2, 1, 3):
                to = rows_at((own_place(role) + d) % 4 * 16, 16, 16)
                over_2[q].append(
                    send(
                        r2_out.at[role, to, columns],
                        r2_in.at[role, d - 1, :, columns],
                        s2.at[q, role, d - 1],
                        near_peer(role, d),
                    )
                )

    def to_planes(q):
        for c in over_2[q]:
            c.wait_recv()
        columns = slice(q * PART, (q + 1) * PART)
        for role in range(2):
            own = r2_own[role, rows_at(own_place(role) * 16, 16, 16), columns]
            for d in range(3):
                own = own + r2_in[role, d, :, columns].astype(F32)
            for j in range(2):
                own_j = own[j * 8:j * 8 + 8]
                r3_own[q, 2 * kinds[role] + j] = own_j
                r3_out[q, 2 * kinds[role] + j] = jnp.concatenate(
                    [own_j[:, :PART // 2], own_j[:, PART // 2:]], axis=0
                ).astype(BF)
        over_3[q] = [
            send(r3_out.at[q, planes[b]], r3_in.at[q, b - 1], s3.at[q, b - 1], (at(x, y, planes[b]), mdl))
            for b in (2, 3, 1)
        ]

    weight_grad(0, act, gate_grad)
    to_near(0)
    to_near(1)
    weight_grad(1, act, up_grad)
    to_planes(0)
    to_planes(1)
    weight_grad(2, grad, down_grad)
    for q in range(PARTS):
        for c in over_3[q]:
            c.wait_recv()
        own = r3_own[q, z]
        for d in range(3):
            got = r3_in[q, d].astype(F32)
            own = own + jnp.concatenate([got[:8], got[8:]], axis=1)
        dx[:, q * PART:(q + 1) * PART] = own

    for c in sent:
        c.wait_send()


def store(dx, gate_grad, up_grad, down_grad, dx_out, gate_out, up_out, down_out, rounded, sem):
    copies = [
        pltpu.make_async_copy(src, dst, sem.at[i])
        for i, (src, dst) in enumerate([(gate_grad, gate_out), (up_grad, up_out), (down_grad, down_out)])
    ]
    for c in copies:
        c.start()
    rounded[...] = dx[...].astype(BF)
    copies.append(pltpu.make_async_copy(rounded, dx_out, sem.at[3]))
    copies[3].start()
    for c in copies:
        c.wait()


def local(
    quant_input, input_scale, grad_output, gate_quant, gate_scale, up_quant, up_scale, down_quant, down_scale,
):
    vmem = pl.BlockSpec(memory_space=pltpu.VMEM)
    hbm = pl.BlockSpec(memory_space=pltpu.HBM)
    dma = pltpu.SemaphoreType.DMA
    weight = jax.ShapeDtypeStruct((H, D), BF)
    dx, gate_grad, up_grad, down_grad = pl.pallas_call(
        kernel,
        name="ffn_backward",
        out_shape=(jax.ShapeDtypeStruct((8, D), F32), weight, weight, weight),
        in_specs=[hbm] * 9,
        out_specs=(vmem,) * 4,
        scratch_shapes=[
            pltpu.VMEM((8, D), BF),
            pltpu.VMEM((8, D), BF),
            pltpu.SMEM((8,), F32),
            pltpu.VMEM((3, 1, H), F32),
            pltpu.VMEM((H, 24), F32),
            pltpu.VMEM((64, 16, D), BF),
            pltpu.VMEM((3, H, D), BF),
            pltpu.VMEM((TOKENS, D), BF),
            pltpu.VMEM((TOKENS, D), BF),
            pltpu.VMEM((TOKENS, 3 * HP), BF),
            pltpu.VMEM((3 * HP, TOKENS), BF),
            pltpu.VMEM((2 * HP, D), BF),
            pltpu.VMEM((HP, D), BF),
            pltpu.VMEM((TOKENS, 3 * HP), F32),
            pltpu.VMEM((TOKENS // 2, 3 * HP), F32),
            pltpu.VMEM((TOKENS // 2, 3 * HP), F32),
            pltpu.VMEM((TOKENS // 2, 11 * 128), BF),
            pltpu.VMEM((TOKENS // 2, 11 * 128), BF),
            pltpu.VMEM((128, D), F32),
            pltpu.VMEM((3, 128, D), BF),
            pltpu.VMEM((2, 3, 64, D), BF),
            pltpu.VMEM((2, 64, D), F32),
            pltpu.VMEM((2, 64, D), BF),
            pltpu.VMEM((2, 3, 16, D), BF),
            pltpu.VMEM((PARTS, 4, 8, PART), F32),
            pltpu.VMEM((PARTS, 4, 16, PART // 2), BF),
            pltpu.VMEM((PARTS, 3, 16, PART // 2), BF),
            dma((9,)),
            dma((3, 2)),
            dma((4, 3, 2)),
            dma((2, 2, 2, 2)),
            dma((2, 2, 2)),
            dma((8, 2)),
            dma((8, 2)),
            dma((8, 2)),
            dma((PARTS, 3, 2, 2, 2)),
            dma((PARTS, 2, 3, 2)),
            dma((PARTS, 3, 2)),
        ],
        compiler_params=pltpu.CompilerParams(
            collective_id=0, has_side_effects=True, vmem_limit_bytes=40 * 2**20
        ),
        cost_estimate=pl.CostEstimate(flops=9 * 10**9, bytes_accessed=12 * 10**6, transcendentals=300000),
    )(
        *(
            pltpu.with_memory_space_constraint(a, pltpu.HBM)
            for a in (
                quant_input, input_scale, grad_output, gate_quant.T, up_quant.T, down_quant,
                gate_scale.reshape(1, H), up_scale.reshape(1, H), down_scale.reshape(1, H),
            )
        )
    )
    dx, gate_grad, up_grad, down_grad = pl.pallas_call(
        store,
        name="store",
        out_shape=(pltpu.HBM((8, D), BF),) + (pltpu.HBM((H, D), BF),) * 3,
        in_specs=[vmem] * 4,
        out_specs=(hbm,) * 4,
        scratch_shapes=[pltpu.VMEM((8, D), BF), dma((4,))],
        compiler_params=pltpu.CompilerParams(vmem_limit_bytes=2**20),
    )(*(pltpu.with_memory_space_constraint(a, pltpu.VMEM) for a in (dx, gate_grad, up_grad, down_grad)))
    return (dx, gate_grad.T, up_grad.T, down_grad)


def solution(mesh):
    in_specs = (
        P("hid", "mdl"),
        P("hid"),
        P("hid", "mdl"),
        P("mdl", "hid"),
        P("hid"),
        P("mdl", "hid"),
        P("hid"),
        P("hid", "mdl"),
        P("hid"),
    )
    out_specs = (P("hid", "mdl"), P("mdl", "hid"), P("mdl", "hid"), P("hid", "mdl"))
    return jax.shard_map(local, mesh=mesh, in_specs=in_specs, out_specs=out_specs, check_vma=False)
```

```python
import jax
import jax.numpy as jnp
from jax import lax
from jax.experimental import pallas as pl
from jax.experimental.pallas import tpu as pltpu
from jax.sharding import PartitionSpec as P

MESH = pl.DeviceIdType.MESH
BF = jnp.bfloat16
F32 = jnp.float32
D = 2048
H = 448
HP = 512
TOKENS = 512
STEP = 64
PARTS = 2
PART = D // PARTS
GROUPS = (
    ((0, 0, 8),),
    ((3, 0, 4), (1, 4, 4)),
    ((2, 0, 8),),
    ((3, 4, 4), (1, 0, 4)),
)


def contract_cols(left, right):
    return lax.dot_general(left, right, (((1,), (1,)), ((), ())), preferred_element_type=F32)


def rows_at(start, size, step):
    return pl.ds(pl.multiple_of(start, step), size)


def packed(s):
    last = s[:, 384:512] + pltpu.roll(s[:, 896:1024], 64, 1)
    return jnp.concatenate([s[:, 0:384], s[:, 512:896], s[:, 1024:1408], last, s[:, 1408:1536]], axis=1)


def unpacked(p):
    shared = p[:, 1152:1280]
    low = lax.broadcasted_iota(jnp.int32, shared.shape, 1) < 64
    gate = jnp.where(low, shared, 0.0)
    up = jnp.where(low, pltpu.roll(shared, 64, 1), 0.0)
    return (
        jnp.concatenate([p[:, 0:384], gate], axis=1),
        jnp.concatenate([p[:, 384:768], up], axis=1),
        jnp.concatenate([p[:, 768:1152], p[:, 1280:1408]], axis=1),
    )


def kernel(
    quant, scale, cotangent, gate_q, up_q, down_q, gate_s, up_s, down_s,
    dx, gate_grad, up_grad, down_grad,
    mine_q, mine_g, mine_s, scale_rows, scales, gathered, raw, act, grad, delta, turned, w_gu, w_d, part, sib, total, z_out, z_in,
    pi_own, pi_out, r1_in, r2_own, r2_out, r2_in, r3_own, r3_out, r3_in,
    load_sem, gz, gp, gn, gf, sc, sz, sd, s1, s2, s3,
):
    hid = lax.axis_index("hid")
    mdl = lax.axis_index("mdl")
    x, z, y = hid % 4, (hid // 4) % 4, hid // 16
    core, half = mdl % 2, mdl // 2
    kinds = (z // 2, 1 - z // 2)

    def at(px, py, pz):
        return (py * 4 + pz) * 4 + px

    def near_peer(role, d):
        k = kinds[role]
        return (at((x + d * (1 - k)) % 4, (y + d * k) % 4, z), mdl)

    def line_peer(role, d):
        k = kinds[role]
        return (at((x + d * k) % 4, (y + d * (1 - k)) % 4, z), mdl)

    planes = (z, z + 1 - 2 * (z % 2), (z + 2) % 4, 3 - z)
    sibling = (hid, half * 2 + (1 - core))
    far = (hid, (1 - half) * 2 + core)

    def place(pz):
        k = pz // 2
        return k * 32 + ((y * 4 + x) * (1 - k) + (x * 4 + y) * k) * 2 + pz % 2

    def line_start(role, ahead):
        k = kinds[role]
        return k * 32 + ((y * (1 - k) + x * k) + ahead) % 4 * 8

    def line(role, ahead, first, size):
        return gathered.at[pl.ds(line_start(role, ahead) + first, size)]

    loads = [
        pltpu.make_async_copy(src, dst, load_sem.at[i])
        for i, (src, dst) in enumerate(
            [(gate_q, raw.at[0]), (up_q, raw.at[1]), (down_q, raw.at[2]), (quant, mine_q), (cotangent, mine_g)]
            + [(scale, mine_s)]
            + [(s, scale_rows.at[i]) for i, s in enumerate((gate_s, up_s, down_s))]
        )
    ]
    for i in (5, 3, 4, 6, 7, 8, 2, 0, 1):
        loads[i].start()

    barrier = pltpu.get_barrier_semaphore()
    partners = [f(0, d) for f in (near_peer, line_peer) for d in (1, 2, 3)]
    partners += [(at(x, y, p), mdl) for p in planes[1:]] + [sibling, far]
    for p in partners:
        pl.semaphore_signal(barrier, inc=1, device_id=p, device_id_type=MESH)

    pos = place(z)
    for i in range(3, 9):
        loads[i].wait()
    row = lax.broadcasted_iota(jnp.int32, (8, 1), 0)
    factor = jnp.zeros((8, 1), F32)
    for i in range(8):
        factor = jnp.where(row == i, mine_s[i], factor)
    gathered[pos] = jnp.concatenate(
        [mine_q[...].astype(F32) * factor, mine_g[...].astype(F32)], axis=0
    ).astype(BF)
    for i in range(3):
        scales[:, 8 * i:8 * i + 8] = jnp.broadcast_to(scale_rows[i], (8, H)).T

    pl.semaphore_wait(barrier, len(partners))

    sent = []

    def send(src, dst, sems, to):
        c = pltpu.make_async_remote_copy(
            src_ref=src, dst_ref=dst, send_sem=sems.at[0], recv_sem=sems.at[1],
            device_id=to, device_id_type=MESH,
        )
        c.start()
        sent.append(c)
        return c

    second = {}

    def over_near(b):
        block = gathered.at[place(planes[b])]
        second[b] = [send(block, block, gp.at[b, e - 1], near_peer(b // 2, e)) for e in (1, 3, 2)]

    over_z = {}

    def to_plane(b):
        own_slab = gathered.at[pos]
        over_z[b] = send(own_slab, own_slab, gz.at[b - 1], (at(x, y, planes[b]), mdl))

    to_plane(1)
    over_near(0)

    def dequantize(i, out, row):
        loads[i].wait()

        @pl.loop(0, 7)
        def _(j):
            r = rows_at(j * 64, 64, 64)
            out[rows_at(row + j * 64, 64, 64), :] = (
                raw[i, r, :].astype(F32) * scales[r, 8 * i:8 * i + 1]
            ).astype(BF)

        out[row + H:row + HP, :] = jnp.zeros((HP - H, D), BF)

    dequantize(2, w_d, 0)
    to_plane(3)
    to_plane(2)
    over_z[1].wait_recv()
    over_near(1)
    dequantize(0, w_gu, 0)
    for b in (3, 2):
        over_z[b].wait_recv()
        over_near(b)
    dequantize(1, w_gu, HP)

    def own_line(role, step):
        out = []
        for i, d in enumerate((1, 3)):
            block = line(role, 0, 4 * (step ^ i), 4)
            out.append(send(block, block, gn.at[step, role, i], line_peer(role, d)))
        return out

    def pass_on(role, arrived):
        for c in arrived:
            c.wait_recv()
        out = []
        for i, d in enumerate((1, 3)):
            block = line(role, 4 - d, 4 * i, 4)
            out.append(send(block, block, gf.at[role, i], line_peer(role, d)))
        return out

    def own_rows(p):
        return rows_at(p * STEP + core * (STEP // 2), STEP // 2, STEP // 2)

    def sums_rows(p):
        return pl.ds(p * (STEP // 2), STEP // 2)

    core_copy, far_copy, ready = {}, {}, {}

    def partials(p):
        start = p * STEP
        for ahead, first, n in GROUPS[p // 2]:
            base = line_start(p % 2, ahead) + first

            @pl.loop(0, n // 2)
            def _(j):
                a = gathered[base + 2 * j].astype(F32)
                b = gathered[base + 2 * j + 1].astype(F32)
                r = rows_at(start + j * 16, 16, 16)
                act[r, :] = jnp.concatenate([a[:8], b[:8]], axis=0).astype(BF)
                grad[r, :] = jnp.concatenate([a[8:], b[8:]], axis=0).astype(BF)

            start += n * 8
        r = pl.ds(p * STEP, STEP)

        @pl.loop(0, 1)
        def _(j):
            c = rows_at(j * 1024, 1024, 1024)
            part[r, c] = contract_cols(act[r, :], w_gu[c, :])

        @pl.loop(0, 1)
        def _(j):
            c = rows_at(j * 512, 512, 512)
            part[r, rows_at(2 * HP + j * 512, 512, 512)] = contract_cols(grad[r, :], w_d[c, :])

        other = rows_at(p * STEP + (1 - core) * (STEP // 2), STEP // 2, STEP // 2)
        core_copy[p] = send(part.at[other], sib.at[sums_rows(p)], sc.at[p], sibling)

    def to_far(p):
        core_copy[p].wait_recv()
        r = sums_rows(p)
        s = part[own_rows(p), :] + sib[r, :]
        total[r, :] = s
        z_out[r, :] = packed(s).astype(BF)
        far_copy[p] = send(z_out.at[r], z_in.at[r], sz.at[p], far)

    def activate(p):
        far_copy[p].wait_recv()
        r = sums_rows(p)
        gate_sum, up_sum, hidden_grad = (
            total[r, i * HP:(i + 1) * HP] + v for i, v in enumerate(unpacked(z_in[r, :].astype(F32)))
        )
        gate_sigmoid = jax.nn.sigmoid(gate_sum)
        mine = own_rows(p)
        delta[mine, 0:HP] = (
            hidden_grad * up_sum * gate_sigmoid * (1.0 + gate_sum * (1.0 - gate_sigmoid))
        ).astype(BF)
        delta[mine, HP:2 * HP] = (hidden_grad * gate_sum * gate_sigmoid).astype(BF)
        delta[mine, 2 * HP:] = (gate_sum * gate_sigmoid * up_sum).astype(BF)
        ready[p] = send(delta.at[mine], delta.at[mine], sd.at[p], sibling)

    over_1 = [[] for _ in range(PARTS)]

    def input_part(k):
        ready[2 * k].wait_recv()
        ready[2 * k + 1].wait_recv()
        r = pl.ds(k * 128, 128)
        for q in range(PARTS):

            @pl.loop(q * PART // 1024, (q + 1) * PART // 1024)
            def _(j):
                c = rows_at(j * 1024, 1024, 1024)
                value = jnp.dot(delta[r, 0:2 * HP], w_gu[:, c], preferred_element_type=F32)
                if k == 0:
                    pi_own[:, c] = value
                else:
                    pi_out[k - 1, :, c] = value.astype(BF)

            if k == 0:
                continue
            row = 0
            columns = slice(q * PART, (q + 1) * PART)
            for role in range(2):
                for i, (ahead, first, size) in enumerate(GROUPS[k]):
                    n = size * 8
                    over_1[q].append(
                        send(
                            pi_out.at[k - 1, row:row + n, columns],
                            r1_in.at[role, {3: 0, 1: 1, 2: 2}[ahead], first * 8:first * 8 + n, columns],
                            s1.at[q, k - 1, role, i],
                            line_peer(role, ahead),
                        )
                    )
                    row += n

    def turn(k):
        r = pl.ds(k * 128, 128)
        for i in range(12):
            turned[i * 128:(i + 1) * 128, r] = delta[r, i * 128:(i + 1) * 128].T

    def weight_grad(i, tokens, out):
        @pl.loop(0, 2)
        def _(j):
            c = rows_at(j * 1024, 1024, 1024)
            out[:, c] = jnp.dot(
                turned[i * HP:i * HP + H, :], tokens[:, c], preferred_element_type=F32
            ).astype(BF)

    third, fourth = {}, {}

    def arrive(copies):
        for c in copies:
            c.wait_recv()

    arrive(second[0] + second[1])
    third[0, 0] = own_line(0, 0)
    partials(0)
    arrive(second[2] + second[3])
    third[1, 0] = own_line(1, 0)
    to_far(0)
    partials(1)
    fourth[0] = pass_on(0, third[0, 0])
    third[0, 1] = own_line(0, 1)
    to_far(1)
    partials(2)
    fourth[1] = pass_on(1, third[1, 0])
    third[1, 1] = own_line(1, 1)
    to_far(2)
    partials(3)
    activate(0)
    to_far(3)
    activate(1)
    arrive(fourth[0])
    partials(4)
    input_part(0)
    to_far(4)
    arrive(fourth[1])
    partials(5)
    turn(0)
    to_far(5)
    arrive(third[0, 1])
    partials(6)
    activate(2)
    to_far(6)
    activate(3)
    arrive(third[1, 1])
    partials(7)
    input_part(1)
    to_far(7)
    activate(4)
    activate(5)
    turn(1)
    input_part(2)
    activate(6)
    activate(7)
    turn(2)
    input_part(3)
    turn(3)

    def own_place(role):
        k = kinds[role]
        return x * (1 - k) + y * k

    over_2, over_3 = {}, {}

    def to_near(q):
        for c in over_1[q]:
            c.wait_recv()
        columns = slice(q * PART, (q + 1) * PART)
        over_2[q] = []
        for role in range(2):
            own = pi_own[role * 64:role * 64 + 64, columns]
            for i in range(3):
                own = own + r1_in[role, i, :, columns].astype(F32)
            r2_own[role, :, columns] = own
            r2_out[role, :, columns] = own.astype(BF)
            for d in (2, 1, 3):
                to = rows_at((own_place(role) + d) % 4 * 16, 16, 16)
                over_2[q].append(
                    send(
                        r2_out.at[role, to, columns],
                        r2_in.at[role, d - 1, :, columns],
                        s2.at[q, role, d - 1],
                        near_peer(role, d),
                    )
                )

    def to_planes(q):
        for c in over_2[q]:
            c.wait_recv()
        columns = slice(q * PART, (q + 1) * PART)
        for role in range(2):
            own = r2_own[role, rows_at(own_place(role) * 16, 16, 16), columns]
            for d in range(3):
                own = own + r2_in[role, d, :, columns].astype(F32)
            for j in range(2):
                own_j = own[j * 8:j * 8 + 8]
                r3_own[q, 2 * kinds[role] + j] = own_j
                r3_out[q, 2 * kinds[role] + j] = jnp.concatenate(
                    [own_j[:, :PART // 2], own_j[:, PART // 2:]], axis=0
                ).astype(BF)
        over_3[q] = [
            send(r3_out.at[q, planes[b]], r3_in.at[q, b - 1], s3.at[q, b - 1], (at(x, y, planes[b]), mdl))
            for b in (2, 3, 1)
        ]

    weight_grad(0, act, gate_grad)
    to_near(0)
    to_near(1)
    weight_grad(1, act, up_grad)
    to_planes(0)
    to_planes(1)
    weight_grad(2, grad, down_grad)
    for q in range(PARTS):
        for c in over_3[q]:
            c.wait_recv()
        own = r3_own[q, z]
        for d in range(3):
            got = r3_in[q, d].astype(F32)
            own = own + jnp.concatenate([got[:8], got[8:]], axis=1)
        dx[:, q * PART:(q + 1) * PART] = own

    for c in sent:
        c.wait_send()


def store(dx, gate_grad, up_grad, down_grad, dx_out, gate_out, up_out, down_out, rounded, sem):
    copies = [
        pltpu.make_async_copy(src, dst, sem.at[i])
        for i, (src, dst) in enumerate([(gate_grad, gate_out), (up_grad, up_out), (down_grad, down_out)])
    ]
    for c in copies:
        c.start()
    rounded[...] = dx[...].astype(BF)
    copies.append(pltpu.make_async_copy(rounded, dx_out, sem.at[3]))
    copies[3].start()
    for c in copies:
        c.wait()


def local(
    quant_input, input_scale, grad_output, gate_quant, gate_scale, up_quant, up_scale, down_quant, down_scale,
):
    vmem = pl.BlockSpec(memory_space=pltpu.VMEM)
    hbm = pl.BlockSpec(memory_space=pltpu.HBM)
    dma = pltpu.SemaphoreType.DMA
    weight = jax.ShapeDtypeStruct((H, D), BF)
    dx, gate_grad, up_grad, down_grad = pl.pallas_call(
        kernel,
        name="ffn_backward",
        out_shape=(jax.ShapeDtypeStruct((8, D), F32), weight, weight, weight),
        in_specs=[hbm] * 9,
        out_specs=(vmem,) * 4,
        scratch_shapes=[
            pltpu.VMEM((8, D), BF),
            pltpu.VMEM((8, D), BF),
            pltpu.SMEM((8,), F32),
            pltpu.VMEM((3, 1, H), F32),
            pltpu.VMEM((H, 24), F32),
            pltpu.VMEM((64, 16, D), BF),
            pltpu.VMEM((3, H, D), BF),
            pltpu.VMEM((TOKENS, D), BF),
            pltpu.VMEM((TOKENS, D), BF),
            pltpu.VMEM((TOKENS, 3 * HP), BF),
            pltpu.VMEM((3 * HP, TOKENS), BF),
            pltpu.VMEM((2 * HP, D), BF),
            pltpu.VMEM((HP, D), BF),
            pltpu.VMEM((TOKENS, 3 * HP), F32),
            pltpu.VMEM((TOKENS // 2, 3 * HP), F32),
            pltpu.VMEM((TOKENS // 2, 3 * HP), F32),
            pltpu.VMEM((TOKENS // 2, 11 * 128), BF),
            pltpu.VMEM((TOKENS // 2, 11 * 128), BF),
            pltpu.VMEM((128, D), F32),
            pltpu.VMEM((3, 128, D), BF),
            pltpu.VMEM((2, 3, 64, D), BF),
            pltpu.VMEM((2, 64, D), F32),
            pltpu.VMEM((2, 64, D), BF),
            pltpu.VMEM((2, 3, 16, D), BF),
            pltpu.VMEM((PARTS, 4, 8, PART), F32),
            pltpu.VMEM((PARTS, 4, 16, PART // 2), BF),
            pltpu.VMEM((PARTS, 3, 16, PART // 2), BF),
            dma((9,)),
            dma((3, 2)),
            dma((4, 3, 2)),
            dma((2, 2, 2, 2)),
            dma((2, 2, 2)),
            dma((8, 2)),
            dma((8, 2)),
            dma((8, 2)),
            dma((PARTS, 3, 2, 2, 2)),
            dma((PARTS, 2, 3, 2)),
            dma((PARTS, 3, 2)),
        ],
        compiler_params=pltpu.CompilerParams(
            collective_id=0, has_side_effects=True, vmem_limit_bytes=40 * 2**20
        ),
        cost_estimate=pl.CostEstimate(flops=9 * 10**9, bytes_accessed=12 * 10**6, transcendentals=300000),
    )(
        *(
            pltpu.with_memory_space_constraint(a, pltpu.HBM)
            for a in (
                quant_input, input_scale, grad_output, gate_quant.T, up_quant.T, down_quant,
                gate_scale.reshape(1, H), up_scale.reshape(1, H), down_scale.reshape(1, H),
            )
        )
    )
    dx, gate_grad, up_grad, down_grad = pl.pallas_call(
        store,
        name="store",
        out_shape=(pltpu.HBM((8, D), BF),) + (pltpu.HBM((H, D), BF),) * 3,
        in_specs=[vmem] * 4,
        out_specs=(hbm,) * 4,
        scratch_shapes=[pltpu.VMEM((8, D), BF), dma((4,))],
        compiler_params=pltpu.CompilerParams(vmem_limit_bytes=2**20),
    )(*(pltpu.with_memory_space_constraint(a, pltpu.VMEM) for a in (dx, gate_grad, up_grad, down_grad)))
    return (dx, gate_grad.T, up_grad.T, down_grad)


def solution(mesh):
    in_specs = (
        P("hid", "mdl"),
        P("hid"),
        P("hid", "mdl"),
        P("mdl", "hid"),
        P("hid"),
        P("mdl", "hid"),
        P("hid"),
        P("hid", "mdl"),
        P("hid"),
    )
    out_specs = (P("hid", "mdl"), P("mdl", "hid"), P("mdl", "hid"), P("hid", "mdl"))
    return jax.shard_map(local, mesh=mesh, in_specs=in_specs, out_specs=out_specs, check_vma=False)
```
